512 devices in a mesh: tm: 32 (over y, x), space: 16 (over z, core).
Axes of the slice: x: 4, y: 8, z: 8, core: 2. Of those that a mesh axis runs over, the one named last changes fastest.
Arguments:
- local_term: float32 [32, 512, 512], P('tm', 'space'), may hold values from -2 to 16, as said below
- coupling: float32 [32, 512, 512], P('tm', 'space'), may hold values from -0.25 to 1.2
Outputs:
- sigma: float32 [32, 512, 512], P('tm', 'space')
The draws below stay inside these ranges and needn't reach their ends.
Inputs may be any that keep to these rules, and one draw needn't show every extreme that they name: local_term[t] is symmetric for every time block t.
All inputs are finite; a program needn't handle non-finite values.
Results may differ from the reference program's by a relative error of at most 0.00014.
Values sent between devices are 32-bit elements; how exact they have to be, the bound alone decides.
No kernel may reach another device: no remote copies, remote signals or barrier semaphores. Data moves between devices by JAX's collectives and lax.ppermute only.
A program may use at most 64 MiB of HBM per device.

```python
import jax
import jax.numpy as jnp
from jax import lax

N = 512
TBLOCKS = 32


def draw_local_term(key, part):
    key_one, key_two = jax.random.split(jax.random.fold_in(key, 11))
    normal_part = jax.random.normal(key_one, (TBLOCKS, N, N), jnp.float32)
    symmetric = (normal_part + jnp.swapaxes(normal_part, 1, 2)) * (0.35 / jnp.sqrt(jnp.float32(N)))
    lower, upper = (1.2, 4.8)
    diagonal = jnp.exp(jax.random.uniform(key_two, (TBLOCKS, N), jnp.float32, jnp.log(lower), jnp.log(upper)))
    return symmetric + diagonal[:, :, None] * jnp.eye(N, dtype=jnp.float32)[None, :, :]


def draw_coupling(key, part):
    key_one, key_two = jax.random.split(jax.random.fold_in(key, 23))
    spread = 0.2 / jnp.sqrt(jnp.float32(N))
    noise = jnp.clip(jax.random.normal(key_one, (TBLOCKS, N, N), jnp.float32), -6.0, 6.0) * spread
    lower, upper = (0.75, 0.95)
    diagonal = jnp.exp(jax.random.uniform(key_two, (TBLOCKS, N), jnp.float32, jnp.log(lower), jnp.log(upper)))
    return noise + diagonal[:, :, None] * jnp.eye(N, dtype=jnp.float32)[None, :, :]


def setup_inputs(seed: int = 0) -> dict:
    streams_of = jax.random.split(jax.random.key(seed), 3)
    local_term = draw_local_term(jax.random.fold_in(streams_of[2], 71), 0)
    coupling = draw_coupling(jax.random.fold_in(streams_of[2], 71), 0)
    return dict(local_term=local_term, coupling=coupling)


def reference(local_term, coupling):
    def backward(later, pair):
        term, cmap = pair
        right = jnp.dot(later, cmap, precision=lax.Precision.HIGHEST, preferred_element_type=jnp.float32)
        current = term + jnp.dot(cmap.T, right, precision=lax.Precision.HIGHEST, preferred_element_type=jnp.float32)
        return current, current

    start = jnp.zeros((N, N), jnp.float32)
    _, sigma = lax.scan(backward, start, (local_term, coupling), reverse=True)
    return sigma
```

```python
import functools

import jax
import jax.numpy as jnp
import numpy as np
from jax import lax
from jax.experimental import pallas as pl
from jax.experimental.pallas import tpu as pltpu
from jax.sharding import Mesh, PartitionSpec as P

AXES = ("yh", "yl", "x", "z", "core")
SIZES = (4, 2, 4, 8, 2)
GROUP = ("yl", "x")
BLOCKS = 32
RADICES = (2, 2, 2, 2, 2)


def site(block):
    return (block % 32) // 8, block % 8


def origin(block, rows):
    return (block % 32) * 16 + rows


def place(block, rows):
    yh, z = site(block)
    core, chip = divmod(rows, 8)
    return int(np.ravel_multi_index((yh, chip // 4, chip % 4, z, core), SIZES))


def move(array, source, target):
    pairs = [(source(t, r), target(t, r)) for t in range(BLOCKS) for r in range(16)]
    return lax.ppermute(array, AXES, pairs)


def split(x):
    high = x.astype(jnp.bfloat16)
    return high, (x - high.astype(jnp.float32)).astype(jnp.bfloat16)


def product(left, right, transposed=False):
    dims = (((1,), (1 if transposed else 0,)), ((), ()))
    high, low = left
    rows = high.shape[0]
    dot = functools.partial(lax.dot_general, dimension_numbers=dims, preferred_element_type=jnp.float32)
    both = dot(jnp.concatenate([high, low], 0), right[0])
    return both[:rows] + both[rows:] + dot(high, right[1])


def combine_kernel(radix, last, info, mine, theirs, first_term, last_map, out, turned):
    core, column = info[0], info[1]

    def halves(slot):
        return [split(half[:, slot].reshape(256, 512)) for half in (mine, theirs)]

    def times(left, right):
        pieces = [product(split(left[:, 256 * i : 256 * i + 256]), right[i]) for i in range(2)]
        return pieces[0] + pieces[1]

    def times_turned(left, right):
        parts = split(left)
        return jnp.concatenate([product(parts, right[i], True) for i in range(2)], 1)

    def ordered(rows):
        return jnp.where(core == 0, rows, jnp.concatenate([rows[:, 256:], rows[:, :256]], 1))

    slab = pl.ds(pl.multiple_of((column // 4) * 128, 128), 128)
    for i, half in enumerate((mine, theirs)):
        turned[:, 256 * i : 256 * i + 256] = half[:, 0, :, slab].reshape(256, 128).T
    left = turned[pl.ds(pl.multiple_of((column % 4) * 32, 32), 32), :]

    maps = [halves(i) for i in range(radix - 1)]
    weighted = []
    for i in range(1, radix):
        weighted.append(times(left, halves(radix - 2 + i)))
        if i < radix - 1:
            left = times_turned(left, maps[i])
    total = None
    chain = last_map[...]
    for i in reversed(range(radix - 1)):
        here = weighted[i] if total is None else weighted[i] + total
        if last:
            total = times(ordered(here), maps[i])
        else:
            both = times(ordered(jnp.concatenate([here, chain], 0)), maps[i])
            total, chain = both[:32], both[32:]
        total = jnp.where(info[2 + i] != 0, total, 0.0)
    term = first_term[...] + total
    if last:
        out[...] = term
    else:
        out[0] = chain
        out[1] = term


def combine(radix, last, info, mine, theirs, first_term, last_map):
    vmem = pl.BlockSpec(memory_space=pltpu.VMEM)
    shape = (32, 512) if last else (2, 32, 512)
    return pl.pallas_call(
        functools.partial(combine_kernel, radix, last),
        out_shape=jax.ShapeDtypeStruct(shape, jnp.float32),
        in_specs=[pl.BlockSpec(memory_space=pltpu.SMEM)] + [vmem] * 4,
        out_specs=vmem,
        scratch_shapes=[pltpu.VMEM((128, 512), jnp.float32)],
        compiler_params=pltpu.CompilerParams(vmem_limit_bytes=48 * 1024 * 1024),
    )(info, mine, theirs, first_term, last_map)


def local(local_term, coupling):
    core = lax.axis_index("core")
    column = core * 8 + lax.axis_index(GROUP)
    end = lax.axis_index("yh") * 8 + lax.axis_index("z")
    both = jnp.concatenate([coupling, local_term], 0)
    length = 1
    for stage, radix in enumerate(RADICES):
        last = stage == len(RADICES) - 1
        if stage == 0:
            windows = [
                move(both, origin, lambda t, r, d=d: place(t + d, r)) for d in reversed(range(radix))
            ]
        else:
            windows = [
                move(both, place, lambda t, r, d=d: place(t + d * length, r)) for d in reversed(range(1, radix))
            ] + [both]
        rows = jnp.stack([w[0] for w in windows[:-1]] + [w[1] for w in windows[1:]])
        mine = lax.all_to_all(jnp.broadcast_to(rows[None], (8,) + rows.shape), GROUP, 0, 0, tiled=True)
        theirs = lax.ppermute(mine, "core", [(0, 1), (1, 0)])
        begin = (end - radix * length + 1) % BLOCKS
        counts = [(begin + i * length < BLOCKS).astype(jnp.int32) for i in range(1, radix)]
        info = jnp.stack([core, column] + counts).astype(jnp.int32)
        both = combine(radix, last, info, mine, theirs, windows[0][1], windows[-1][0])
        length *= radix
    return move(both, lambda t, r: place(t + BLOCKS - 1, r), origin)[None]


def solution(mesh):
    fine = Mesh(mesh.devices.reshape(SIZES), AXES)
    spec = P(("yh", "yl", "x"), ("z", "core"), None)
    return jax.shard_map(local, mesh=fine, in_specs=(spec, spec), out_specs=spec, check_vma=False)
```

```python
import functools

import jax
import jax.numpy as jnp
import numpy as np
from jax import lax
from jax.experimental import pallas as pl
from jax.experimental.pallas import tpu as pltpu
from jax.sharding import Mesh, PartitionSpec as P

AXES = ("yh", "yl", "x", "zh", "zl", "core")
SIZES = (4, 2, 4, 4, 2, 2)
GROUP = ("yl", "x")
BLOCKS = 32
LEVELS = 5


def site(block):
    bit = [(block >> i) & 1 for i in range(5)]
    return 2 * bit[0] + bit[3], 2 * bit[2] + bit[1], bit[4]


def origin(block, rows):
    return (block % BLOCKS) * 16 + rows


def place(block, rows):
    yh, zh, zl = site(block % BLOCKS)
    core, chip = divmod(rows, 8)
    return int(np.ravel_multi_index((yh, chip // 4, chip % 4, zh, zl, core), SIZES))


def move(array, source, target):
    pairs = [(source(t, r), target(t, r)) for t in range(BLOCKS) for r in range(16)]
    return lax.ppermute(array, AXES, pairs)


def split(x):
    high = x.astype(jnp.bfloat16)
    return high, (x - high.astype(jnp.float32)).astype(jnp.bfloat16)


def product(left, right):
    high, low = left
    rows = high.shape[0]
    dot = functools.partial(jnp.dot, preferred_element_type=jnp.float32)
    both = dot(jnp.concatenate([high, low], 0), right[0])
    return both[:rows] + both[rows:] + dot(high, right[1])


def combine_kernel(last, info, mine, theirs, term, *refs):
    core, column, map_slot, term_slot, counts = (info[i] for i in range(5))
    turned = refs[-1]

    def times(left, slot):
        pieces = [
            product(split(left[:, 256 * i : 256 * i + 256]), split(half[:, slot].reshape(256, 512)))
            for i, half in enumerate((mine, theirs))
        ]
        return pieces[0] + pieces[1]

    def ordered(rows):
        return jnp.where(core == 0, rows, jnp.concatenate([rows[:, 256:], rows[:, :256]], 1))

    slab = pl.ds(pl.multiple_of((column // 4) * 128, 128), 128)
    for i, half in enumerate((mine, theirs)):
        turned[:, 256 * i : 256 * i + 256] = half[:, map_slot, :, slab].reshape(256, 128).T
    left = turned[pl.ds(pl.multiple_of((column % 4) * 32, 32), 32), :]
    weighted = times(left, term_slot)
    if last:
        out = refs[0]
        total = times(ordered(weighted), map_slot)
        out[...] = term[...] + jnp.where(counts != 0, total, 0.0)
    else:
        later_map, out = refs[0], refs[1]
        both = times(ordered(jnp.concatenate([weighted, later_map[...]], 0)), map_slot)
        out[0] = both[32:]
        out[1] = term[...] + jnp.where(counts != 0, both[:32], 0.0)


def combine(last, info, *arrays):
    vmem = pl.BlockSpec(memory_space=pltpu.VMEM)
    shape = (32, 512) if last else (2, 32, 512)
    return pl.pallas_call(
        functools.partial(combine_kernel, last),
        out_shape=jax.ShapeDtypeStruct(shape, jnp.float32),
        in_specs=[pl.BlockSpec(memory_space=pltpu.SMEM)] + [vmem] * len(arrays),
        out_specs=vmem,
        scratch_shapes=[pltpu.VMEM((128, 512), jnp.float32)],
        compiler_params=pltpu.CompilerParams(vmem_limit_bytes=32 * 1024 * 1024),
    )(jnp.stack(info).astype(jnp.int32), *arrays)


def local(local_term, coupling):
    core, yh, zh, zl = (lax.axis_index(a) for a in ("core", "yh", "zh", "zl"))
    column = core * 8 + lax.axis_index(GROUP)
    end = yh // 2 + 2 * (zh % 2) + 4 * (zh // 2) + 8 * (yh % 2) + 16 * zl
    both = jnp.concatenate([coupling, local_term], 0)
    for level in range(LEVELS - 1):
        length = 1 << level
        if level == 0:
            earlier = move(both, origin, lambda t, r: place(t + 1, r))
            own = move(both, origin, place)
        else:
            own = both
            earlier = move(both, place, lambda t, r: place(t + length, r))
        rows = jnp.stack([earlier[0], own[1]])
        mine = lax.all_to_all(jnp.broadcast_to(rows[None], (8, 2, 32, 512)), GROUP, 0, 0, tiled=True)
        theirs = lax.ppermute(mine, "core", [(0, 1), (1, 0)])
        counts = (end - 2 * length + 1) % BLOCKS + length < BLOCKS
        both = combine(False, [core, column, 0, 1, counts], mine, theirs, earlier[1], own[0])

    is_earlier = (end - 15) % BLOCKS < 16
    rows = jnp.where(is_earlier, both[0], both[1])
    mine = lax.all_to_all(jnp.broadcast_to(rows[None], (16, 32, 512)), GROUP + ("zl",), 0, 0, tiled=True)
    mine = mine.reshape(8, 2, 32, 512)
    theirs = lax.ppermute(mine, "core", [(0, 1), (1, 0)])
    map_slot = jnp.where(is_earlier, zl, 1 - zl)
    term = combine(True, [core, column, map_slot, 1 - map_slot, is_earlier], mine, theirs, both[1])
    return move(term, lambda t, r: place(t + 15, r), origin)[None]


def solution(mesh):
    fine = Mesh(mesh.devices.reshape(SIZES), AXES)
    spec = P(("yh", "yl", "x"), ("zh", "zl", "core"), None)
    return jax.shard_map(local, mesh=fine, in_specs=(spec, spec), out_specs=spec, check_vma=False)
```

```python
import functools

import jax
import jax.numpy as jnp
import numpy as np
from jax import lax
from jax.experimental import pallas as pl
from jax.experimental.pallas import tpu as pltpu
from jax.sharding import Mesh, PartitionSpec as P

AXES = ("yh", "yl", "xh", "xl", "zh", "zl", "core")
SIZES = (4, 2, 2, 2, 4, 2, 2)
GROUP = ("yl", "xl", "xh")
BLOCKS = 32
LEVELS = 5


def site(block):
    bit = [(block >> i) & 1 for i in range(5)]
    return 2 * bit[2] + bit[1], 2 * bit[0] + bit[3], bit[4]


def origin(block, rows):
    return (block % BLOCKS) * 16 + rows


def place(block, rows):
    yh, zh, zl = site(block % BLOCKS)
    core, chip = divmod(rows, 8)
    return int(np.ravel_multi_index((yh, chip // 4, chip % 2, chip // 2 % 2, zh, zl, core), SIZES))


def move(array, source, target):
    pairs = [(source(t, r), target(t, r)) for t in range(BLOCKS) for r in range(16)]
    return lax.ppermute(array, AXES, pairs)


def split(x):
    high = x.astype(jnp.bfloat16)
    return high, (x - high.astype(jnp.float32)).astype(jnp.bfloat16)


def product(left, right, transposed=False):
    high, low = left
    rows = high.shape[0]
    dims = (((1,), (1 if transposed else 0,)), ((), ()))
    dot = functools.partial(lax.dot_general, dimension_numbers=dims, preferred_element_type=jnp.float32)
    both = dot(jnp.concatenate([high, low], 0), right[0])
    return both[:rows] + both[rows:] + dot(high, right[1])


def blocks(halves, at, width):
    found = []
    for half in halves:
        high, low = split(half[:, :, at : at + width].reshape(256, width))
        found += [(high[:128], low[:128]), (high[128:], low[128:])]
    return found


def rows_of_map(column, halves, turned):
    slab = pl.ds(pl.multiple_of((column // 4) * 128, 128), 128)
    for i, half in enumerate(halves):
        turned[:, 256 * i : 256 * i + 256] = half(slab).reshape(256, 128).T
    return turned[pl.ds(pl.multiple_of((column % 4) * 32, 32), 32), :]


def own_first(core, rows):
    return jnp.where(core == 0, rows, jnp.concatenate([rows[:, 256:], rows[:, :256]], 1))


def times(left, halves):
    pieces = [
        product(split(left[:, 256 * i : 256 * i + 256]), split(half.reshape(256, 512))) for i, half in enumerate(halves)
    ]
    return pieces[0] + pieces[1]


def level_kernel(info, mine, theirs, term, later_map, out, sent, turned, twice):
    core, column, counts = info[0], info[1], info[2]
    halves = (mine, theirs)
    left = rows_of_map(column, [lambda at, half=half: half[:, :, at] for half in halves], turned)
    lefts = [split(left[:, 128 * i : 128 * i + 128]) for i in range(4)]
    stored = blocks(halves, 512, 384)
    weighted = [0.0] * 4
    for i in range(4):
        row = product(lefts[i], stored[i])
        for j in range(3):
            weighted[(i + j) % 4] += row[:, 128 * j : 128 * j + 128]
        above = tuple(part[:, 128:256] for part in stored[i])
        weighted[i] += product(lefts[(i + 1) % 4], above, True)
    left = jnp.concatenate([jnp.concatenate(weighted, 1), own_first(core, later_map[...])], 0)
    both = times(left, [half[:, :, :512] for half in halves])
    total = term[...] + jnp.where(counts != 0, both[:32], 0.0)
    out[0] = both[32:]
    out[1] = total
    twice[:, :512] = total
    twice[:, 512:] = total
    sent[...] = twice[:, pl.ds(pl.multiple_of((column // 4) * 128, 128), 384)]


def last_kernel(info, mine, theirs, term, out, turned):
    core, column, map_slot, term_slot, counts = (info[i] for i in range(5))
    halves = (mine, theirs)
    left = rows_of_map(column, [lambda at, half=half: half[:, map_slot, :, at] for half in halves], turned)
    weighted = times(left, [half[:, term_slot] for half in halves])
    total = times(own_first(core, weighted), [half[:, map_slot] for half in halves])
    out[...] = term[...] + jnp.where(counts != 0, total, 0.0)


def call(kernel, shapes, widths, info, *arrays):
    vmem = pl.BlockSpec(memory_space=pltpu.VMEM)
    return pl.pallas_call(
        kernel,
        out_shape=[jax.ShapeDtypeStruct(shape, jnp.float32) for shape in shapes],
        in_specs=[pl.BlockSpec(memory_space=pltpu.SMEM)] + [vmem] * len(arrays),
        out_specs=[vmem] * len(shapes),
        scratch_shapes=[pltpu.VMEM(shape, jnp.float32) for shape in widths],
        compiler_params=pltpu.CompilerParams(vmem_limit_bytes=32 * 1024 * 1024),
    )(jnp.stack(info).astype(jnp.int32), *arrays)


def local(local_term, coupling):
    core, yh, zh, zl = (lax.axis_index(a) for a in ("core", "yh", "zh", "zl"))
    column = core * 8 + lax.axis_index(GROUP)
    end = zh // 2 + 2 * (yh % 2) + 4 * (yh // 2) + 8 * (zh % 2) + 16 * zl
    both = jnp.concatenate([coupling, local_term], 0)
    for level in range(LEVELS - 1):
        length = 1 << level
        if level == 0:
            earlier = move(both, origin, lambda t, r: place(t + 1, r))
            own = move(both, origin, place)
            sent = lax.dynamic_slice_in_dim(jnp.tile(own[1], (1, 2)), column // 4 * 128, 384, 1)
        else:
            own = both
            earlier = move(both, place, lambda t, r: place(t + length, r))
        rows = jnp.concatenate([earlier[0], sent], 1)
        mine = lax.all_to_all(jnp.broadcast_to(rows[None], (8, 32, 896)), GROUP, 0, 0, tiled=True)
        theirs = lax.ppermute(mine, "core", [(0, 1), (1, 0)])
        counts = (end - 2 * length + 1) % BLOCKS + length < BLOCKS
        both, sent = call(
            level_kernel,
            [(2, 32, 512), (32, 384)],
            [(128, 512), (32, 1024)],
            [core, column, counts],
            *(mine, theirs, earlier[1], own[0]),
        )

    is_earlier = (end - 15) % BLOCKS < 16
    rows = jnp.where(is_earlier, both[0], both[1])
    mine = lax.all_to_all(jnp.broadcast_to(rows[None], (16, 32, 512)), GROUP + ("zl",), 0, 0, tiled=True)
    mine = mine.reshape(8, 2, 32, 512)
    theirs = lax.ppermute(mine, "core", [(0, 1), (1, 0)])
    map_slot = jnp.where(is_earlier, zl, 1 - zl)
    info = [core, column, map_slot, 1 - map_slot, is_earlier]
    (term,) = call(last_kernel, [(32, 512)], [(128, 512)], info, mine, theirs, both[1])
    return move(term, lambda t, r: place(t + 15, r), origin)[None]


def solution(mesh):
    fine = Mesh(mesh.devices.reshape(SIZES), AXES)
    spec = P(("yh", "yl", "xh", "xl"), ("zh", "zl", "core"), None)
    return jax.shard_map(local, mesh=fine, in_specs=(spec, spec), out_specs=spec, check_vma=False)
```

```python
import functools

import jax
import jax.numpy as jnp
import numpy as np
from jax import lax
from jax.experimental import pallas as pl
from jax.experimental.pallas import tpu as pltpu
from jax.sharding import Mesh, PartitionSpec as P

AXES = ("yh", "yl", "xh", "xl", "zh", "zl", "core")
SIZES = (4, 2, 2, 2, 4, 2, 2)
GROUP = ("xl", "zl", "xh")
BLOCKS = 32
LEVELS = 5


def site(block):
    bit = [(block >> i) & 1 for i in range(5)]
    return 2 * bit[2] + bit[1], bit[4], 2 * bit[0] + bit[3]


def origin(block, rows):
    return (block % BLOCKS) * 16 + rows


def place(block, rows):
    yh, yl, zh = site(block % BLOCKS)
    core, chip = divmod(rows, 8)
    return int(np.ravel_multi_index((yh, yl, chip % 2, chip // 4, zh, chip // 2 % 2, core), SIZES))


def move(array, source, target):
    pairs = [(source(t, r), target(t, r)) for t in range(BLOCKS) for r in range(16)]
    return lax.ppermute(array, AXES, pairs)


def split(x):
    high = x.astype(jnp.bfloat16)
    return high, (x - high.astype(jnp.float32)).astype(jnp.bfloat16)


def product(left, right, transposed=False):
    high, low = left
    rows = high.shape[0]
    dims = (((1,), (1 if transposed else 0,)), ((), ()))
    dot = functools.partial(lax.dot_general, dimension_numbers=dims, preferred_element_type=jnp.float32)
    both = dot(jnp.concatenate([high, low], 0), right[0])
    return both[:rows] + both[rows:] + dot(high, right[1])


def blocks(halves, at, width):
    found = []
    for half in halves:
        high, low = split(half[:, :, at : at + width].reshape(256, width))
        found += [(high[:128], low[:128]), (high[128:], low[128:])]
    return found


def rows_of_map(column, halves, turned):
    slab = pl.ds(pl.multiple_of((column // 4) * 128, 128), 128)
    for i, half in enumerate(halves):
        turned[:, 256 * i : 256 * i + 256] = half(slab).reshape(256, 128).T
    return turned[pl.ds(pl.multiple_of((column % 4) * 32, 32), 32), :]


def own_first(core, rows):
    return jnp.where(core == 0, rows, jnp.concatenate([rows[:, 256:], rows[:, :256]], 1))


def times(left, halves):
    pieces = [
        product(split(left[:, 256 * i : 256 * i + 256]), split(half.reshape(256, 512))) for i, half in enumerate(halves)
    ]
    return pieces[0] + pieces[1]


def level_kernel(before_last, info, mine, theirs, term, later_map, out, sent, turned, twice):
    core, column, counts = info[0], info[1], info[2]
    halves = (mine, theirs)
    left = rows_of_map(column, [lambda at, half=half: half[:, :, at] for half in halves], turned)
    lefts = [split(left[:, 128 * i : 128 * i + 128]) for i in range(4)]
    stored = blocks(halves, 512, 384)
    weighted = [0.0] * 4
    for i in range(4):
        row = product(lefts[i], stored[i])
        for j in range(3):
            weighted[(i + j) % 4] += row[:, 128 * j : 128 * j + 128]
        above = tuple(part[:, 128:256] for part in stored[i])
        weighted[i] += product(lefts[(i + 1) % 4], above, True)
    left = jnp.concatenate([jnp.concatenate(weighted, 1), own_first(core, later_map[...])], 0)
    both = times(left, [half[:, :, :512] for half in halves])
    total = term[...] + jnp.where(counts != 0, both[:32], 0.0)
    if before_last:
        out[...] = total
        sent[...] = jnp.where(info[3] != 0, both[32:], total)
        return
    out[0] = both[32:]
    out[1] = total
    twice[:, :512] = total
    twice[:, 512:] = total
    sent[...] = twice[:, pl.ds(pl.multiple_of((column // 4) * 128, 128), 384)]


def last_kernel(info, mine, theirs, term, out, turned):
    core, column, map_slot, term_slot, counts = (info[i] for i in range(5))
    halves = (mine, theirs)
    left = rows_of_map(column, [lambda at, half=half: half[:, map_slot, :, at] for half in halves], turned)
    weighted = times(left, [half[:, term_slot] for half in halves])
    total = times(own_first(core, weighted), [half[:, map_slot] for half in halves])
    out[...] = term[...] + jnp.where(counts != 0, total, 0.0)


def call(kernel, shapes, widths, info, *arrays):
    vmem = pl.BlockSpec(memory_space=pltpu.VMEM)
    return pl.pallas_call(
        kernel,
        out_shape=[jax.ShapeDtypeStruct(shape, jnp.float32) for shape in shapes],
        in_specs=[pl.BlockSpec(memory_space=pltpu.SMEM)] + [vmem] * len(arrays),
        out_specs=[vmem] * len(shapes),
        scratch_shapes=[pltpu.VMEM(shape, jnp.float32) for shape in widths],
        compiler_params=pltpu.CompilerParams(vmem_limit_bytes=32 * 1024 * 1024),
    )(jnp.stack(info).astype(jnp.int32), *arrays)


def local(local_term, coupling):
    core, yh, zh, yl = (lax.axis_index(a) for a in ("core", "yh", "zh", "yl"))
    column = core * 8 + lax.axis_index(GROUP)
    end = zh // 2 + 2 * (yh % 2) + 4 * (yh // 2) + 8 * (zh % 2) + 16 * yl
    is_earlier = (end - 15) % BLOCKS < 16
    both = jnp.concatenate([coupling, local_term], 0)
    for level in range(LEVELS - 1):
        length = 1 << level
        if level == 0:
            earlier = move(both, origin, lambda t, r: place(t + 1, r))
            own = move(both, origin, place)
            sent = lax.dynamic_slice_in_dim(jnp.tile(own[1], (1, 2)), column // 4 * 128, 384, 1)
        else:
            own = both
            earlier = move(both, place, lambda t, r: place(t + length, r))
        rows = jnp.concatenate([earlier[0], sent], 1)
        mine = lax.all_to_all(jnp.broadcast_to(rows[None], (8, 32, 896)), GROUP, 0, 0, tiled=True)
        theirs = lax.ppermute(mine, "core", [(0, 1), (1, 0)])
        counts = (end - 2 * length + 1) % BLOCKS + length < BLOCKS
        before_last = level == LEVELS - 2
        both, sent = call(
            functools.partial(level_kernel, before_last),
            [(32, 512), (32, 512)] if before_last else [(2, 32, 512), (32, 384)],
            [(128, 512), (32, 1024)],
            [core, column, counts, is_earlier],
            *(mine, theirs, earlier[1], own[0]),
        )

    mine = lax.all_to_all(jnp.broadcast_to(sent[None], (16, 32, 512)), GROUP + ("yl",), 0, 0, tiled=True)
    mine = mine.reshape(8, 2, 32, 512)
    theirs = lax.ppermute(mine, "core", [(0, 1), (1, 0)])
    map_slot = jnp.where(is_earlier, yl, 1 - yl)
    info = [core, column, map_slot, 1 - map_slot, is_earlier]
    (term,) = call(last_kernel, [(32, 512)], [(128, 512)], info, mine, theirs, both)
    return move(term, lambda t, r: place(t + 15, r), origin)[None]


def solution(mesh):
    fine = Mesh(mesh.devices.reshape(SIZES), AXES)
    spec = P(("yh", "yl", "xh", "xl"), ("zh", "zl", "core"), None)
    return jax.shard_map(local, mesh=fine, in_specs=(spec, spec), out_specs=spec, check_vma=False)
```

```python
import functools

import jax
import jax.numpy as jnp
import numpy as np
from jax import lax
from jax.experimental import pallas as pl
from jax.experimental.pallas import tpu as pltpu
from jax.sharding import Mesh, PartitionSpec as P

AXES = ("yh", "yl", "xh", "xl", "zh", "zl", "core")
SIZES = (4, 2, 2, 2, 4, 2, 2)
GROUP = ("xl", "zl", "xh")
BLOCKS = 32
LEVELS = 5


def site(block):
    bit = [(block >> i) & 1 for i in range(5)]
    return 2 * bit[2] + bit[1], bit[4], 2 * bit[0] + bit[3]


def origin(block, rows):
    return (block % BLOCKS) * 16 + rows


def place(block, rows):
    yh, yl, zh = site(block % BLOCKS)
    core, chip = divmod(rows, 8)
    return int(np.ravel_multi_index((yh, yl, chip % 2, chip // 4, zh, chip // 2 % 2, core), SIZES))


def move(array, source, target):
    pairs = [(source(t, r), target(t, r)) for t in range(BLOCKS) for r in range(16)]
    return lax.ppermute(array, AXES, pairs)


def split(x):
    high = x.astype(jnp.bfloat16)
    return high, (x - high.astype(jnp.float32)).astype(jnp.bfloat16)


def product(left, right, transposed=False):
    high, low = left
    rows = high.shape[0]
    dims = (((1,), (1 if transposed else 0,)), ((), ()))
    dot = functools.partial(lax.dot_general, dimension_numbers=dims, preferred_element_type=jnp.float32)
    both = dot(jnp.concatenate([high, low], 0), right[0])
    return both[:rows] + both[rows:] + dot(high, right[1])


def blocks(halves, at, width):
    found = []
    for half in halves:
        high, low = split(half[:, :, at : at + width].reshape(256, width))
        found += [(high[:128], low[:128]), (high[128:], low[128:])]
    return found


def rows_of_map(column, halves, turned):
    slab = pl.ds(pl.multiple_of((column // 4) * 128, 128), 128)
    for i, half in enumerate(halves):
        turned[:, 256 * i : 256 * i + 256] = half(slab).reshape(256, 128).T
    return turned[pl.ds(pl.multiple_of((column % 4) * 32, 32), 32), : 256 * len(halves)]


def own_first(core, rows):
    return jnp.where(core == 0, rows, jnp.concatenate([rows[:, 256:], rows[:, :256]], 1))


def times(left, halves):
    pieces = [
        product(split(left[:, 256 * i : 256 * i + 256]), split(half.reshape(256, 512))) for i, half in enumerate(halves)
    ]
    return pieces[0] + pieces[1]


def early_kernel(info, mine, later_map, out_left, out_weighted, out_map, turned):
    core, column = info[0], info[1]
    left = rows_of_map(column, [lambda at: mine[:, :, at]], turned)
    lefts = [split(left[:, 128 * i : 128 * i + 128]) for i in range(2)]
    stored = blocks([mine], 512, 384)
    weighted = [0.0] * 4
    for i in range(2):
        row = product(lefts[i], stored[i])
        for j in range(3):
            weighted[i + j] += row[:, 128 * j : 128 * j + 128]
    weighted[0] += product(lefts[1], tuple(part[:, 128:256] for part in stored[0]), True)
    out_left[...] = left
    out_weighted[...] = jnp.concatenate(weighted, 1)
    own = own_first(core, later_map[...])[:, :256]
    out_map[...] = product(split(own), split(mine[:, :, :512].reshape(256, 512)))


def level_kernel(before_last, info, mine, theirs, term, later_map, early_left, early_weighted, early_map, out, sent, turned, twice):
    core, column, counts = info[0], info[1], info[2]
    left = jnp.concatenate([early_left[...], rows_of_map(column, [lambda at: theirs[:, :, at]], turned)], 1)
    lefts = [split(left[:, 128 * i : 128 * i + 128]) for i in range(4)]
    stored = blocks([theirs], 512, 384)
    weighted = [early_weighted[:, 128 * i : 128 * i + 128] for i in range(4)]
    for i in (2, 3):
        row = product(lefts[i], stored[i - 2])
        for j in range(3):
            weighted[(i + j) % 4] += row[:, 128 * j : 128 * j + 128]
    high, low = split(mine[4:, :, 640:768].reshape(128, 128))
    weighted[1] += product(lefts[2], (high, low), True)
    for i in (2, 3):
        above = tuple(part[:, 128:256] for part in stored[i - 2])
        weighted[i] += product(lefts[(i + 1) % 4], above, True)
    own = jnp.concatenate(weighted[:2], 1)
    other = jnp.concatenate([jnp.concatenate(weighted[2:], 1), own_first(core, later_map[...])[:, 256:]], 0)
    total = product(split(own), split(mine[:, :, :512].reshape(256, 512)))
    both = product(split(other), split(theirs[:, :, :512].reshape(256, 512)))
    total = term[...] + jnp.where(counts != 0, total + both[:32], 0.0)
    new_map = early_map[...] + both[32:]
    if before_last:
        out[...] = total
        sent[...] = jnp.where(info[3] != 0, new_map, total)
        return
    out[0] = new_map
    out[1] = total
    twice[:, :512] = total
    twice[:, 512:] = total
    sent[...] = twice[:, pl.ds(pl.multiple_of((column // 4) * 128, 128), 384)]


def last_kernel(info, mine, theirs, term, out, turned):
    core, column, map_slot, term_slot, counts = (info[i] for i in range(5))
    halves = (mine, theirs)
    left = rows_of_map(column, [lambda at, half=half: half[:, map_slot, :, at] for half in halves], turned)
    weighted = times(left, [half[:, term_slot] for half in halves])
    total = times(own_first(core, weighted), [half[:, map_slot] for half in halves])
    out[...] = term[...] + jnp.where(counts != 0, total, 0.0)


def call(kernel, shapes, widths, info, *arrays):
    vmem = pl.BlockSpec(memory_space=pltpu.VMEM)
    return pl.pallas_call(
        kernel,
        out_shape=[jax.ShapeDtypeStruct(shape, jnp.float32) for shape in shapes],
        in_specs=[pl.BlockSpec(memory_space=pltpu.SMEM)] + [vmem] * len(arrays),
        out_specs=[vmem] * len(shapes),
        scratch_shapes=[pltpu.VMEM(shape, jnp.float32) for shape in widths],
        compiler_params=pltpu.CompilerParams(vmem_limit_bytes=32 * 1024 * 1024),
    )(jnp.stack(info).astype(jnp.int32), *arrays)


def local(local_term, coupling):
    core, yh, zh, yl = (lax.axis_index(a) for a in ("core", "yh", "zh", "yl"))
    column = core * 8 + lax.axis_index(GROUP)
    end = zh // 2 + 2 * (yh % 2) + 4 * (yh // 2) + 8 * (zh % 2) + 16 * yl
    is_earlier = (end - 15) % BLOCKS < 16
    both = jnp.concatenate([coupling, local_term], 0)
    for level in range(LEVELS - 1):
        length = 1 << level
        if level == 0:
            earlier = move(both, origin, lambda t, r: place(t + 1, r))
            own = move(both, origin, place)
            sent = lax.dynamic_slice_in_dim(jnp.tile(own[1], (1, 2)), column // 4 * 128, 384, 1)
        else:
            own = both
            earlier = move(both, place, lambda t, r: place(t + length, r))
        rows = jnp.concatenate([earlier[0], sent], 1)
        mine = lax.all_to_all(jnp.broadcast_to(rows[None], (8, 32, 896)), GROUP, 0, 0, tiled=True)
        theirs = lax.ppermute(mine, "core", [(0, 1), (1, 0)])
        counts = (end - 2 * length + 1) % BLOCKS + length < BLOCKS
        before_last = level == LEVELS - 2
        info = [core, column, counts, is_earlier]
        early = call(
            early_kernel, [(32, 256), (32, 512), (32, 512)], [(128, 256)], info, mine, own[0]
        )
        both, sent = call(
            functools.partial(level_kernel, before_last),
            [(32, 512), (32, 512)] if before_last else [(2, 32, 512), (32, 384)],
            [(128, 256), (32, 1024)],
            info,
            *(mine, theirs, earlier[1], own[0], *early),
        )

    mine = lax.all_to_all(jnp.broadcast_to(sent[None], (16, 32, 512)), GROUP + ("yl",), 0, 0, tiled=True)
    mine = mine.reshape(8, 2, 32, 512)
    theirs = lax.ppermute(mine, "core", [(0, 1), (1, 0)])
    map_slot = jnp.where(is_earlier, yl, 1 - yl)
    info = [core, column, map_slot, 1 - map_slot, is_earlier]
    (term,) = call(last_kernel, [(32, 512)], [(128, 512)], info, mine, theirs, both)
    return move(term, lambda t, r: place(t + 15, r), origin)[None]


def solution(mesh):
    fine = Mesh(mesh.devices.reshape(SIZES), AXES)
    spec = P(("yh", "yl", "xh", "xl"), ("zh", "zl", "core"), None)
    return jax.shard_map(local, mesh=fine, in_specs=(spec, spec), out_specs=spec, check_vma=False)
```

```python
import functools

import jax
import jax.numpy as jnp
import numpy as np
from jax import lax
from jax.experimental import pallas as pl
from jax.experimental.pallas import tpu as pltpu
from jax.sharding import Mesh, PartitionSpec as P

AXES = ("yh", "yl", "xh", "xl", "zh", "zl", "core")
SIZES = (4, 2, 2, 2, 4, 2, 2)
GROUP = ("xl", "zl", "xh")
BLOCKS = 32
LEVELS = 5


def site(block):
    bit = [(block >> i) & 1 for i in range(5)]
    return 2 * bit[2] + bit[1], bit[4], 2 * bit[0] + bit[3]


def origin(block, rows):
    return (block % BLOCKS) * 16 + rows


def place(block, rows):
    yh, yl, zh = site(block % BLOCKS)
    core, chip = divmod(rows, 8)
    return int(np.ravel_multi_index((yh, yl, chip % 2, chip // 4, zh, chip // 2 % 2, core), SIZES))


def move(array, source, target):
    pairs = [(source(t, r), target(t, r)) for t in range(BLOCKS) for r in range(16)]
    return lax.ppermute(array, AXES, pairs)


def split(x):
    high = x.astype(jnp.bfloat16)
    return high, (x - high.astype(jnp.float32)).astype(jnp.bfloat16)


def product(left, right, transposed=False):
    high, low = left
    rows = high.shape[0]
    dims = (((1,), (1 if transposed else 0,)), ((), ()))
    dot = functools.partial(lax.dot_general, dimension_numbers=dims, preferred_element_type=jnp.float32)
    both = dot(jnp.concatenate([high, low], 0), right[0])
    return both[:rows] + both[rows:] + dot(high, right[1])


def blocks(halves, at, width):
    found = []
    for half in halves:
        high, low = split(half[:, :, at : at + width].reshape(256, width))
        found += [(high[:128], low[:128]), (high[128:], low[128:])]
    return found


def rows_of_map(column, halves, turned):
    slab = pl.ds(pl.multiple_of((column // 4) * 128, 128), 128)
    for i, half in enumerate(halves):
        turned[:, 256 * i : 256 * i + 256] = half(slab).reshape(256, 128).T
    return turned[pl.ds(pl.multiple_of((column % 4) * 32, 32), 32), : 256 * len(halves)]


def own_first(core, rows):
    return jnp.where(core == 0, rows, jnp.concatenate([rows[:, 256:], rows[:, :256]], 1))


def times(left, halves):
    pieces = [
        product(split(left[:, 256 * i : 256 * i + 256]), split(half.reshape(256, 512))) for i, half in enumerate(halves)
    ]
    return pieces[0] + pieces[1]


def early_kernel(info, mine, later_map, out, turned):
    core, column = info[0], info[1]
    left = rows_of_map(column, [lambda at: mine[:, :, at]], turned)
    lefts = [split(left[:, 128 * i : 128 * i + 128]) for i in range(2)]
    stored = blocks([mine], 512, 384)
    weighted = [0.0] * 4
    for i in range(2):
        row = product(lefts[i], stored[i])
        for j in range(3):
            weighted[i + j] += row[:, 128 * j : 128 * j + 128]
    weighted[0] += product(lefts[1], tuple(part[:, 128:256] for part in stored[0]), True)
    out[:, :256] = left
    out[:, 256:768] = jnp.concatenate(weighted, 1)
    own = own_first(core, later_map[...])[:, :256]
    out[:, 768:] = product(split(own), split(mine[:, :, :512].reshape(256, 512)))


def level_kernel(before_last, info, mine, theirs, term, later_map, early, out, sent, turned, twice):
    core, column, counts = info[0], info[1], info[2]
    left = jnp.concatenate([early[:, :256], rows_of_map(column, [lambda at: theirs[:, :, at]], turned)], 1)
    lefts = [split(left[:, 128 * i : 128 * i + 128]) for i in range(4)]
    stored = blocks([theirs], 512, 384)
    weighted = [early[:, 256 + 128 * i : 384 + 128 * i] for i in range(4)]
    for i in (2, 3):
        row = product(lefts[i], stored[i - 2])
        for j in range(3):
            weighted[(i + j) % 4] += row[:, 128 * j : 128 * j + 128]
    high, low = split(mine[4:, :, 640:768].reshape(128, 128))
    weighted[1] += product(lefts[2], (high, low), True)
    for i in (2, 3):
        above = tuple(part[:, 128:256] for part in stored[i - 2])
        weighted[i] += product(lefts[(i + 1) % 4], above, True)
    own = jnp.concatenate(weighted[:2], 1)
    other = jnp.concatenate([jnp.concatenate(weighted[2:], 1), own_first(core, later_map[...])[:, 256:]], 0)
    total = product(split(own), split(mine[:, :, :512].reshape(256, 512)))
    both = product(split(other), split(theirs[:, :, :512].reshape(256, 512)))
    total = term[...] + jnp.where(counts != 0, total + both[:32], 0.0)
    new_map = early[:, 768:] + both[32:]
    if before_last:
        out[...] = total
        sent[...] = jnp.where(info[3] != 0, new_map, total)
        return
    out[0] = new_map
    out[1] = total
    twice[:, :512] = total
    twice[:, 512:] = total
    sent[...] = twice[:, pl.ds(pl.multiple_of((column // 4) * 128, 128), 384)]


def last_kernel(info, mine, theirs, term, out, turned):
    core, column, map_slot, term_slot, counts = (info[i] for i in range(5))
    halves = (mine, theirs)
    left = rows_of_map(column, [lambda at, half=half: half[:, map_slot, :, at] for half in halves], turned)
    weighted = times(left, [half[:, term_slot] for half in halves])
    total = times(own_first(core, weighted), [half[:, map_slot] for half in halves])
    out[...] = term[...] + jnp.where(counts != 0, total, 0.0)


def call(kernel, shapes, widths, info, *arrays):
    vmem = pl.BlockSpec(memory_space=pltpu.VMEM)
    return pl.pallas_call(
        kernel,
        out_shape=[jax.ShapeDtypeStruct(shape, jnp.float32) for shape in shapes],
        in_specs=[pl.BlockSpec(memory_space=pltpu.SMEM)] + [vmem] * len(arrays),
        out_specs=[vmem] * len(shapes),
        scratch_shapes=[pltpu.VMEM(shape, jnp.float32) for shape in widths],
        compiler_params=pltpu.CompilerParams(vmem_limit_bytes=32 * 1024 * 1024),
    )(jnp.stack(info).astype(jnp.int32), *arrays)


def local(local_term, coupling):
    core, yh, zh, yl = (lax.axis_index(a) for a in ("core", "yh", "zh", "yl"))
    column = core * 8 + lax.axis_index(GROUP)
    end = zh // 2 + 2 * (yh % 2) + 4 * (yh // 2) + 8 * (zh % 2) + 16 * yl
    is_earlier = (end - 15) % BLOCKS < 16
    both = jnp.concatenate([coupling, local_term], 0)
    for level in range(LEVELS - 1):
        length = 1 << level
        if level == 0:
            earlier = move(both, origin, lambda t, r: place(t + 1, r))
            own = move(both, origin, place)
            sent = lax.dynamic_slice_in_dim(jnp.tile(own[1], (1, 2)), column // 4 * 128, 384, 1)
        else:
            own = both
            earlier = move(both, place, lambda t, r: place(t + length, r))
        rows = jnp.concatenate([earlier[0], sent], 1)
        mine = lax.all_to_all(jnp.broadcast_to(rows[None], (8, 32, 896)), GROUP, 0, 0, tiled=True)
        theirs = lax.ppermute(mine, "core", [(0, 1), (1, 0)])
        counts = (end - 2 * length + 1) % BLOCKS + length < BLOCKS
        before_last = level == LEVELS - 2
        info = [core, column, counts, is_earlier]
        early = call(
            early_kernel, [(32, 1280)], [(128, 256)], info, mine, own[0]
        )
        both, sent = call(
            functools.partial(level_kernel, before_last),
            [(32, 512), (32, 512)] if before_last else [(2, 32, 512), (32, 384)],
            [(128, 256), (32, 1024)],
            info,
            *(mine, theirs, earlier[1], own[0], *early),
        )

    mine = lax.all_to_all(jnp.broadcast_to(sent[None], (16, 32, 512)), GROUP + ("yl",), 0, 0, tiled=True)
    mine = mine.reshape(8, 2, 32, 512)
    theirs = lax.ppermute(mine, "core", [(0, 1), (1, 0)])
    map_slot = jnp.where(is_earlier, yl, 1 - yl)
    info = [core, column, map_slot, 1 - map_slot, is_earlier]
    (term,) = call(last_kernel, [(32, 512)], [(128, 512)], info, mine, theirs, both)
    return move(term, lambda t, r: place(t + 15, r), origin)[None]


def solution(mesh):
    fine = Mesh(mesh.devices.reshape(SIZES), AXES)
    spec = P(("yh", "yl", "xh", "xl"), ("zh", "zl", "core"), None)
    return jax.shard_map(local, mesh=fine, in_specs=(spec, spec), out_specs=spec, check_vma=False)
```
